32 devices in a mesh: seq: 8 (over z, x), head: 4 (over y, core).
Axes of the slice: x: 2, y: 2, z: 4, core: 2. Of those that a mesh axis runs over, the one named last changes fastest.
Arguments:
- queries: bfloat16 [2, 2048, 2048], P(None, 'seq', 'head'), may hold values from -1.75 to 1.75
- keys: bfloat16 [2, 2048, 2048], P(None, 'seq', 'head'), may hold values from -1.75 to 1.75
- values: bfloat16 [2, 2048, 2048], P(None, 'seq', 'head'), may hold values from -6 to 6
- gate_pre: bfloat16 [2, 2048, 2048], P(None, 'seq', 'head'), may hold values from -8 to 8
- grad_out: bfloat16 [2, 2048, 4096], P(None, 'seq', 'head'), may hold values from -6 to 6
- w_query: bfloat16 [4096, 2048], P(None, 'head'), may hold values from -0.09375 to 0.09375
- w_key: bfloat16 [4096, 2048], P(None, 'head'), may hold values from -0.09375 to 0.09375
- w_value: bfloat16 [4096, 2048], P(None, 'head'), may hold values from -0.09375 to 0.09375
- w_gate: bfloat16 [4096, 2048], P(None, 'head'), may hold values from -0.09375 to 0.09375
- w_out: bfloat16 [2048, 4096], P('head'), may hold values from -0.125 to 0.125
Outputs:
- grad_in: bfloat16 [2, 2048, 4096], P(None, 'seq', 'head')
The draws below stay inside these ranges and needn't reach their ends.
All inputs are finite; a program needn't handle non-finite values.
Results may differ from the reference program's by a relative error of at most 0.022.
Values may be sent and summed in bfloat16 or wider, within the bound.
A program may use at most 128 MiB of HBM per device.

```python
import jax
import jax.numpy as jnp
from jax import lax

D = 4096
HD = 128
HEADS = 16
SPAN = 256
SEQS = 2
LENGTH = 2048
N_HEAD = 4


def levels(stream_key, shape, split, least, high):
    factor_of, own = 1.0, jax.random.fold_in(stream_key, 6)
    for axis_at, shards_of in split:
        draws = jnp.exp(jax.random.uniform(jax.random.fold_in(own, axis_at), (shards_of,), jnp.float32, least / len(split), high / len(split)))
        factor_of = factor_of * jnp.repeat(draws, shape[axis_at] // shards_of).reshape([-1 if axis == axis_at else 1 for axis in range(len(shape))])
    return factor_of


def gaussian(rng, dims, spread, reach, shards=(), kind=jnp.bfloat16):
    entries = jax.random.normal(rng, dims, jnp.float32) * spread
    if len(shards) > 0:
        entries = levels(rng, dims, shards, -0.22, 0.18) * entries
    return jnp.clip(entries, min=-reach, max=reach).astype(kind)


def setup_inputs(seed: int = 0) -> dict:
    seeds = jax.random.split(jax.random.key(seed), 11)
    return {
        "queries": gaussian(seeds[0], (SEQS, LENGTH, HEADS * HD), 0.3, 1.75, ((1, 8), (2, 4))),
        "keys": gaussian(seeds[1], (SEQS, LENGTH, HEADS * HD), 0.3, 1.75, ((1, 8), (2, 4))),
        "values": gaussian(seeds[2], (SEQS, LENGTH, HEADS * HD), 1.0, 6.0, ((1, 8), (2, 4))),
        "gate_pre": gaussian(seeds[3], (SEQS, LENGTH, HEADS * HD), 1.5, 8.0, ((1, 8), (2, 4))),
        "grad_out": gaussian(seeds[4], (SEQS, LENGTH, D), 1.0, 6.0, ((1, 8), (2, 4))),
        "w_query": gaussian(seeds[5], (D, HEADS * HD), D ** -0.5, 0.09375, ((1, 4),)),
        "w_key": gaussian(seeds[6], (D, HEADS * HD), D ** -0.5, 0.09375, ((1, 4),)),
        "w_value": gaussian(seeds[7], (D, HEADS * HD), D ** -0.5, 0.09375, ((1, 4),)),
        "w_gate": gaussian(seeds[8], (D, HEADS * HD), D ** -0.5, 0.09375, ((1, 4),)),
        "w_out": gaussian(seeds[9], (HEADS * HD, D), (HEADS * HD) ** -0.5, 0.125, ((0, 4),)),
    }


def product(pattern, former, latter):
    return jnp.einsum(pattern, former.astype(jnp.float32), latter.astype(jnp.float32), precision=lax.Precision.HIGHEST)


def rounded(tensor):
    return lax.optimization_barrier(tensor.astype(jnp.bfloat16)).astype(jnp.float32)


def head_blocks(operands):
    queries, keys, values, d_output = operands
    factor = LENGTH ** -0.5
    causal = jnp.tril(jnp.ones((SPAN, SPAN), dtype=bool))
    key_state = product("snck,sncv->snkv", keys, values)
    query_state = product("snck,sncv->snkv", queries, d_output)
    zero_block = jnp.zeros_like(key_state[:, :1])
    prefix = jnp.concatenate([zero_block, jnp.cumsum(key_state, axis=1)[:, :-1]], axis=1)
    after = jnp.flip(jnp.cumsum(jnp.flip(query_state, 1), axis=1), 1)
    suffix = jnp.concatenate([after[:, 1:], zero_block], axis=1)
    scores = rounded(jnp.where(causal, product("sntk,snuk->sntu", queries, keys), 0.0))
    backward = rounded(jnp.where(causal, product("sntv,snuv->sntu", d_output, values), 0.0))
    attended = factor * (product("sntk,snkv->sntv", queries, prefix) + product("sntu,snuv->sntv", scores, values))
    d_query = factor * (product("sntv,snkv->sntk", d_output, prefix) + product("sntu,snuk->sntk", backward, keys))
    d_key = factor * (product("sntu,sntk->snuk", backward, queries) + product("snuv,snkv->snuk", values, suffix))
    d_value = factor * (product("sntu,sntv->snuv", scores, d_output) + product("snuk,snkv->snuv", keys, suffix))
    return attended, d_query.astype(jnp.bfloat16), d_key.astype(jnp.bfloat16), d_value.astype(jnp.bfloat16)


def reference(queries, keys, values, gate_pre, grad_out, w_query, w_key, w_value, w_gate, w_out):
    blocks = LENGTH // SPAN
    columns = HEADS * HD
    d_gated = jnp.dot(grad_out.reshape(SEQS * LENGTH, D), w_out.T, preferred_element_type=jnp.float32).reshape(SEQS, LENGTH, columns)
    gate_open = jax.nn.sigmoid(gate_pre.astype(jnp.float32))
    d_output = (d_gated * gate_open).astype(jnp.bfloat16)

    def to_heads(tensor):
        return jnp.transpose(tensor.reshape(SEQS, blocks, SPAN, HEADS, HD), (3, 0, 1, 2, 4))

    def from_heads(tensor):
        return jnp.transpose(tensor, (1, 2, 3, 0, 4)).reshape(SEQS, LENGTH, columns)

    results = lax.map(head_blocks, (to_heads(queries), to_heads(keys), to_heads(values), to_heads(d_output)))
    attended, d_query, d_key, d_value = [from_heads(stacked) for stacked in results]
    d_gate = (d_gated * attended * gate_open * (1.0 - gate_open)).astype(jnp.bfloat16)
    group_cols = columns // N_HEAD

    def by_group(tensor):
        return jnp.transpose(tensor.reshape(SEQS * LENGTH, N_HEAD, group_cols), (1, 0, 2))

    def weight_group(weight):
        return jnp.transpose(weight.reshape(D, N_HEAD, group_cols), (1, 2, 0))

    grads = tuple(by_group(tensor) for tensor in (d_query, d_key, d_value, d_gate))
    weights = tuple(weight_group(weight) for weight in (w_query, w_key, w_value, w_gate))

    def add_group(running, slices):
        grad_parts, weight_parts = slices
        partial_sum = jnp.zeros((SEQS * LENGTH, D), jnp.float32)
        for grad_part, weight_part in zip(grad_parts, weight_parts):
            partial_sum = partial_sum + jnp.dot(grad_part, weight_part, preferred_element_type=jnp.float32)
        return running + rounded(partial_sum), None

    total, unused = lax.scan(add_group, jnp.zeros((SEQS * LENGTH, D), jnp.float32), (grads, weights))
    return total.astype(jnp.bfloat16).reshape(SEQS, LENGTH, D)
```

```python
import functools

import jax
import jax.numpy as jnp
from jax import lax
from jax.experimental import pallas as pl
from jax.experimental.pallas import tpu as pltpu
from jax.sharding import PartitionSpec as P

HD = 128
TILE = 256
MESH = pl.DeviceIdType.MESH
BF16, F32 = jnp.bfloat16, jnp.float32


def dot(a, b, ca, cb):
    return lax.dot_general(a, b, (((ca,), (cb,)), ((), ())), preferred_element_type=F32)


def kernel(
    n, ns,
    q_h, k_h, v_h, g_h, go_h, wq_h, wk_h, wv_h, wg_h, wo_h, out_ref,
    q_v, k_v, v_v, g_v, wo_v, w_v, gbuf, sc, att, dgated, dout, dcat, dki, dvi, acc,
    ks_send, ks_pair, ks_sum, ks_slots, qs_send, qs_pair, qs_sum, qs_slots, state,
    part_send, part_recv, y_send, y_recv, own,
    ld, ld_own, ag_s, ag_f, ag_r, kp, kg_s, kg_r, qp, qg_s, qg_r, ps, pr, ys, yr,
):
    seqs, span, cols = q_v.shape
    feat = go_h.shape[2]
    width = wq_h.shape[0]
    heads = cols // HD
    chips, groups = n // 2, ns // 2
    factor = float(ns * span) ** (-0.5)
    i, j = lax.axis_index("seq"), lax.axis_index("head")
    c, p = j // 2, lax.rem(j, 2)
    g, r = i // 2, lax.rem(i, 2)
    pj, pi = j + 1 - 2 * p, i + 1 - 2 * r
    others = [lax.rem(c + d, chips) for d in range(1, chips)]

    def rc(src, dst, ss, rs, dev):
        return pltpu.make_async_remote_copy(
            src_ref=src, dst_ref=dst, send_sem=ss, recv_sem=rs, device_id=dev, device_id_type=MESH
        )

    barrier = pltpu.get_barrier_semaphore()
    peers = [(i, pj), (pi, j)]
    peers += [(i, 2 * o + p) for o in others]
    peers += [(2 * lax.rem(g + d, groups) + r, j) for d in range(1, groups)]
    for peer in peers:
        pl.semaphore_signal(barrier, inc=1, device_id=peer, device_id_type=MESH)

    pairs = [(k_h, k_v), (v_h, v_v), (q_h, q_v), (wo_h, wo_v), (g_h, g_v)]
    pairs += [(w, w_v.at[x]) for x, w in enumerate((wq_h, wg_h, wk_h, wv_h))]
    loads = [pltpu.make_async_copy(a, b, ld.at[x]) for x, (a, b) in enumerate(pairs)]
    own_loads = [pltpu.make_async_copy(go_h.at[s], gbuf.at[s, j], ld_own.at[s]) for s in range(seqs)]
    for load in loads[:4] + own_loads + loads[4:]:
        load.start()
    pl.semaphore_wait(barrier, len(peers))

    def ag_far(s):
        return [
            rc(go_h.at[s], gbuf.at[s, j], ag_s.at[s, x], ag_r.at[s, j], (i, 2 * o + p))
            for x, o in enumerate(others)
        ]

    def ag_near(s):
        return rc(go_h.at[s], gbuf.at[s, j], ag_s.at[s, chips - 1], ag_r.at[s, j], (i, pj))

    def ag_wait(s, src):
        rc(go_h.at[s], gbuf.at[s, src], ag_s.at[s, 0], ag_r.at[s, src], (i, pj)).wait_recv()

    far = [ag_far(s) for s in range(seqs)]
    near = [ag_near(s) for s in range(seqs)]
    for copy in far[0]:
        copy.start()
    near[0].start()

    def lane(h):
        return slice(h * HD, (h + 1) * HD)

    def pair_copy(src, dst, sem, s):
        return rc(src.at[s], dst.at[s], sem.at[0, s], sem.at[1, s], (pi, j))

    def group_copy(src, dst, ss, rs, s, to):
        return rc(src.at[s], dst.at[s, g], ss.at[s, to], rs.at[s, g], (2 * to + r, j))

    def spread(send, pair, total, slots, ps_, ss, rs, s, later):
        pair_copy(send, pair, ps_, s).wait_recv()
        for h in range(heads):
            total[s, h] = (send[s, h].astype(F32) + pair[s, h].astype(F32)).astype(BF16)
        for to in range(groups):
            @pl.when((to > g) if later else (to < g))
            def _():
                group_copy(total, slots, ss, rs, s, to).start()

    def spread_end(send, pair, total, slots, ps_, ss, rs, s, later):
        pair_copy(send, pair, ps_, s).wait_send()
        for to in range(groups):
            @pl.when((to > g) if later else (to < g))
            def _():
                group_copy(total, slots, ss, rs, s, to).wait_send()

    def gather_state(pair, slots, ss, rs, total, s, earlier):
        for h in range(heads):
            state[h] = jnp.where(r == (1 if earlier else 0), pair[s, h].astype(F32), 0.0)
        for frm in range(groups):
            @pl.when((frm < g) if earlier else (frm > g))
            def _():
                rc(total.at[s], slots.at[s, frm], ss.at[s, frm], rs.at[s, frm], (pi, j)).wait_recv()
                for h in range(heads):
                    state[h] += slots[s, frm, h].astype(F32)

    kargs = (ks_send, ks_pair, ks_sum, ks_slots, kp, kg_s, kg_r)
    qargs = (qs_send, qs_pair, qs_sum, qs_slots, qp, qg_s, qg_r)

    loads[0].wait()
    loads[1].wait()
    for s in range(seqs):
        for h in range(heads):
            ks_send[s, h] = dot(k_v[s, :, lane(h)], v_v[s, :, lane(h)], 0, 0).astype(BF16)
        pair_copy(ks_send, ks_pair, kp, s).start()

    rows = lax.broadcasted_iota(jnp.int32, (span, span), 0)
    causal = rows >= lax.broadcasted_iota(jnp.int32, (span, span), 1)

    loads[2].wait()
    for s in range(seqs):
        for h in range(heads):
            score = dot(q_v[s, :, lane(h)], k_v[s, :, lane(h)], 1, 1)
            score = jnp.where(causal, score, 0.0).astype(BF16)
            sc[s, h] = score
            att[s, :, lane(h)] = dot(score, v_v[s, :, lane(h)], 1, 0)
        spread(*kargs, s, True)
    loads[3].wait()
    loads[4].wait()

    def gated(s, src, first=False):
        at = pl.ds(pl.multiple_of(src * feat, feat), feat)
        new = dot(gbuf[s, src], wo_v[:, at], 1, 1)
        if first:
            dgated[...] = new
        else:
            dgated[...] += new

    def stage_b(s):
        own_loads[s].wait()
        gated(s, j, True)
        ag_wait(s, pj)
        gated(s, pj)
        if s + 1 < seqs:
            for copy in far[s]:
                copy.wait_send()
            for copy in far[s + 1]:
                copy.start()
            near[s + 1].start()
        for x, o in enumerate(others):
            src = 2 * o + p
            ag_wait(s, src)
            rc(gbuf.at[s, src], gbuf.at[s, src], ag_f.at[s, x], ag_r.at[s, src], (i, pj)).start()
            gated(s, src)
        for o in others:
            src = 2 * o + 1 - p
            ag_wait(s, src)
            gated(s, src)
        for h in range(heads):
            gate = jax.nn.sigmoid(g_v[s, :, lane(h)].astype(F32))
            d_out = (dgated[:, lane(h)] * gate).astype(BF16)
            dout[s, :, lane(h)] = d_out
            qs_send[s, h] = dot(q_v[s, :, lane(h)], d_out, 0, 0).astype(BF16)
        pair_copy(qs_send, qs_pair, qp, s).start()
        gather_state(ks_pair, ks_slots, kg_s, kg_r, ks_sum, s, True)
        for h in range(heads):
            query, key, value = q_v[s, :, lane(h)], k_v[s, :, lane(h)], v_v[s, :, lane(h)]
            d_out = dout[s, :, lane(h)]
            back = jnp.where(causal, dot(d_out, value, 1, 1), 0.0).astype(BF16)
            prefix = state[h].astype(BF16)
            dq = dot(back, key, 1, 0) + dot(d_out, prefix, 1, 1)
            dcat[0, s, :, lane(h)] = (factor * dq).astype(BF16)
            dki[s, :, lane(h)] = dot(back, query, 0, 0)
            dvi[s, :, lane(h)] = dot(sc[s, h], d_out, 0, 0)
            attended = factor * (att[s, :, lane(h)] + dot(query, prefix, 1, 0))
            gate = jax.nn.sigmoid(g_v[s, :, lane(h)].astype(F32))
            d_gate = dgated[:, lane(h)] * attended * gate * (1.0 - gate)
            dcat[1, s, :, lane(h)] = d_gate.astype(BF16)
        spread(*qargs, s, False)

    def half(s, at, lo):
        return dot(dcat[lo, s], w_v[lo, at, :], 1, 1) + dot(dcat[lo + 1, s], w_v[lo + 1, at, :], 1, 1)

    def early(s):
        def step(t, carry):
            at = pl.ds(pl.multiple_of(t * TILE, TILE), TILE)
            acc[:, at] = half(s, at, 0)
            return carry

        lax.fori_loop(0, width // TILE, step, 0)

    def tiles(s, chunk, started, put):
        def step(t, carry):
            at = pl.ds(pl.multiple_of(chunk * feat + t * TILE, TILE), TILE)
            to = pl.ds(pl.multiple_of(t * TILE, TILE), TILE)
            new = half(s, at, 2)
            put(to, new + (acc[:, at] if started else half(s, at, 0)))
            return carry

        lax.fori_loop(0, feat // TILE, step, 0)

    def part_copy(s, o):
        return rc(part_send.at[s, o], part_recv.at[s, o], ps.at[s, o], pr.at[s, o], (i, pj))

    def y_copy(s, o):
        return rc(y_send.at[s, o], y_recv.at[s, c], ys.at[s, o], yr.at[s, c], (i, 2 * o + p))

    def stage_c(s, started):
        gather_state(qs_pair, qs_slots, qg_s, qg_r, qs_sum, s, False)
        for h in range(heads):
            suffix = state[h].astype(BF16)
            dk = dki[s, :, lane(h)] + dot(v_v[s, :, lane(h)], suffix, 1, 1)
            dv = dvi[s, :, lane(h)] + dot(k_v[s, :, lane(h)], suffix, 1, 0)
            dcat[2, s, :, lane(h)] = (factor * dk).astype(BF16)
            dcat[3, s, :, lane(h)] = (factor * dv).astype(BF16)
        for o in others:
            def put(to, new):
                part_send[s, o, :, to] = new.astype(BF16)

            tiles(s, 2 * o + 1 - p, started, put)
            part_copy(s, o).start()
        for o in others:
            part_copy(s, o).wait_recv()

            def put(to, new):
                y_send[s, o, :, to] = (new + part_recv[s, o, :, to].astype(F32)).astype(BF16)

            tiles(s, 2 * o + p, started, put)
            y_copy(s, o).start()

        def put(to, new):
            part_send[s, c, :, to] = new.astype(BF16)

        tiles(s, 2 * c + 1 - p, started, put)
        part_copy(s, c).start()

        def put_own(to, new):
            own[s, :, to] = new

        tiles(s, j, started, put_own)

    def finish(s):
        part_copy(s, c).wait_recv()
        own[s] += part_recv[s, c].astype(F32)
        for o in others:
            rc(y_send.at[s, o], y_recv.at[s, o], ys.at[s, o], yr.at[s, o], (i, 2 * o + p)).wait_recv()
            own[s] += y_recv[s, o].astype(F32)
        out_ref[s] = own[s].astype(BF16)

    stage_b(0)
    for load in loads[5:]:
        load.wait()
    early(0)
    for s in range(1, seqs):
        stage_b(s)
    for s in range(seqs):
        stage_c(s, s == 0)
    for s in range(seqs):
        finish(s)

    for copy in far[seqs - 1]:
        copy.wait_send()
    for s in range(seqs):
        near[s].wait_send()
        for x, o in enumerate(others):
            src = 2 * o + p
            rc(gbuf.at[s, src], gbuf.at[s, src], ag_f.at[s, x], ag_r.at[s, src], (i, pj)).wait_send()
        spread_end(*kargs, s, True)
        spread_end(*qargs, s, False)
        for o in others:
            part_copy(s, o).wait_send()
            y_copy(s, o).wait_send()
        part_copy(s, c).wait_send()


def body(n, ns, queries, keys, values, gate_pre, grad_out, w_query, w_key, w_value, w_gate, w_out):
    seqs, span, cols = queries.shape
    feat, width = grad_out.shape[2], w_query.shape[0]
    heads, chips, groups = cols // HD, n // 2, ns // 2
    vm = pltpu.VMEM
    dma = pltpu.SemaphoreType.DMA
    tok = (seqs, span, cols)
    st = (seqs, heads, HD, HD)
    slots = (seqs, groups, heads, HD, HD)
    chunk = (seqs, chips, span, feat)
    scratch = [
        vm(tok, BF16), vm(tok, BF16), vm(tok, BF16), vm(tok, BF16),
        vm(w_out.shape, BF16), vm((4, width, cols), BF16),
        vm((seqs, n, span, feat), BF16),
        vm((seqs, heads, span, span), BF16), vm(tok, F32), vm((span, cols), F32),
        vm(tok, BF16), vm((4,) + tok, BF16), vm(tok, F32), vm(tok, F32), vm((span, width), F32),
        vm(st, BF16), vm(st, BF16), vm(st, BF16), vm(slots, BF16),
        vm(st, BF16), vm(st, BF16), vm(st, BF16), vm(slots, BF16),
        vm((heads, HD, HD), F32),
        vm(chunk, BF16), vm(chunk, BF16), vm(chunk, BF16), vm(chunk, BF16),
        vm((seqs, span, feat), F32),
        dma((9,)), dma((seqs,)), dma((seqs, chips)), dma((seqs, chips)), dma((seqs, n)),
        dma((2, seqs)), dma((seqs, groups)), dma((seqs, groups)),
        dma((2, seqs)), dma((seqs, groups)), dma((seqs, groups)),
        dma((seqs, chips)), dma((seqs, chips)), dma((seqs, chips)), dma((seqs, chips)),
    ]
    flops = 2 * seqs * span * cols * width * 5
    return pl.pallas_call(
        functools.partial(kernel, n, ns),
        out_shape=jax.ShapeDtypeStruct((seqs, span, feat), BF16),
        in_specs=[pl.BlockSpec(memory_space=pl.ANY)] * 10,
        out_specs=pl.BlockSpec(memory_space=pltpu.VMEM),
        scratch_shapes=scratch,
        cost_estimate=pl.CostEstimate(flops=flops, bytes_accessed=10 * width * cols, transcendentals=0),
        compiler_params=pltpu.CompilerParams(
            collective_id=0, has_side_effects=True, vmem_limit_bytes=58 * 1024 * 1024
        ),
    )(queries, keys, values, gate_pre, grad_out, w_query, w_key, w_value, w_gate, w_out)


def solution(mesh):
    return jax.shard_map(
        functools.partial(body, mesh.shape["head"], mesh.shape["seq"]),
        mesh=mesh,
        in_specs=(
            P(None, "seq", "head"),
            P(None, "seq", "head"),
            P(None, "seq", "head"),
            P(None, "seq", "head"),
            P(None, "seq", "head"),
            P(None, "head"),
            P(None, "head"),
            P(None, "head"),
            P(None, "head"),
            P("head", None),
        ),
        out_specs=P(None, "seq", "head"),
        check_vma=False,
    )
```

```python
import functools

import jax
import jax.numpy as jnp
from jax import lax
from jax.experimental import pallas as pl
from jax.experimental.pallas import tpu as pltpu
from jax.sharding import PartitionSpec as P

HD = 128
TILE = 256
MESH = pl.DeviceIdType.MESH
BF16, F32 = jnp.bfloat16, jnp.float32


def dot(a, b, ca, cb):
    return lax.dot_general(a, b, (((ca,), (cb,)), ((), ())), preferred_element_type=F32)


def kernel(
    n, ns,
    q_h, k_h, v_h, g_h, go_h, wq_h, wk_h, wv_h, wg_h, wo_h, own_h, y_h,
    q_v, k_v, v_v, g_v, wo_v, w_v, gbuf, sc, att, dgated, dout, dcat, dki, dvi, acc,
    ks_send, ks_pair, ks_sum, ks_slots, ks_z, qs_send, qs_pair, qs_sum, qs_slots, qs_z, state,
    part_send, part_recv, y_send, own, own_b,
    ld, ld_own, ag_s, ag_f, ag_r, kp, kg_s, kg_r, kz, qp, qg_s, qg_r, qz, ps, pr, ys, yr, ow,
):
    seqs, span, cols = q_v.shape
    feat = go_h.shape[2]
    width = wq_h.shape[0]
    heads = cols // HD
    hs = heads // 2
    chips, groups = n // 2, ns // 2
    factor = float(ns * span) ** (-0.5)
    i, j = lax.axis_index("seq"), lax.axis_index("head")
    c, p = j // 2, lax.rem(j, 2)
    g, r = i // 2, lax.rem(i, 2)
    pj, pi = j + 1 - 2 * p, i + 1 - 2 * r
    others = [lax.rem(c + d, chips) for d in range(1, chips)]

    def rc(src, dst, ss, rs, dev):
        return pltpu.make_async_remote_copy(
            src_ref=src, dst_ref=dst, send_sem=ss, recv_sem=rs, device_id=dev, device_id_type=MESH
        )

    barrier = pltpu.get_barrier_semaphore()
    peers = [(i, pj), (pi, j)]
    peers += [(i, 2 * o + p) for o in others]
    peers += [(2 * lax.rem(g + d, groups) + r, j) for d in range(1, groups)]
    for peer in peers:
        pl.semaphore_signal(barrier, inc=1, device_id=peer, device_id_type=MESH)

    pairs = [(k_h, k_v), (v_h, v_v), (q_h, q_v), (wo_h, wo_v), (g_h, g_v)]
    pairs += [(w, w_v.at[x]) for x, w in enumerate((wq_h, wg_h, wk_h, wv_h))]
    loads = [pltpu.make_async_copy(a, b, ld.at[x]) for x, (a, b) in enumerate(pairs)]
    own_loads = [pltpu.make_async_copy(go_h.at[s], gbuf.at[s, j], ld_own.at[s]) for s in range(seqs)]
    for load in loads[:4] + own_loads + loads[4:]:
        load.start()
    pl.semaphore_wait(barrier, len(peers))

    def ag_far(s):
        return [
            rc(go_h.at[s], gbuf.at[s, j], ag_s.at[s, x], ag_r.at[s, j], (i, 2 * o + p))
            for x, o in enumerate(others)
        ]

    def ag_near(s):
        return rc(go_h.at[s], gbuf.at[s, j], ag_s.at[s, chips - 1], ag_r.at[s, j], (i, pj))

    def ag_wait(s, src):
        rc(go_h.at[s], gbuf.at[s, src], ag_s.at[s, 0], ag_r.at[s, src], (i, pj)).wait_recv()

    far = [ag_far(s) for s in range(seqs)]
    near = [ag_near(s) for s in range(seqs)]
    for copy in far[0]:
        copy.start()
    near[0].start()

    def lane(h):
        return slice(h * HD, (h + 1) * HD)

    def pair_copy(a, s, m):
        half = r if m else 1 - r
        return rc(a[0].at[s, half], a[1].at[s, half], a[5].at[0, s, m], a[5].at[1, s, m], (pi, j))

    def group_copy(a, s, to):
        return rc(a[2].at[s], a[3].at[s, g], a[6].at[s, to], a[7].at[s, g], (2 * to + r, j))

    def z_copy(a, s):
        return rc(a[4].at[s, r], a[4].at[s, r], a[8].at[0, s], a[8].at[1, s], (pi, j))

    def send_pair(a, s):
        pair_copy(a, s, 0).start()
        pair_copy(a, s, 1).start()

    def relay_p(a, s):
        pair_copy(a, s, 0).wait_recv()
        for k in range(hs):
            a[2][s, k] = (a[0][s, r, k].astype(F32) + a[1][s, r, k].astype(F32)).astype(BF16)
        for to in range(groups):
            @pl.when((to > g) if a[9] else (to < g))
            def _():
                group_copy(a, s, to).start()

    def relay_z(a, s):
        for k in range(hs):
            state[k] = jnp.zeros((HD, HD), F32)
        for frm in range(groups):
            @pl.when((frm < g) if a[9] else (frm > g))
            def _():
                rc(a[2].at[s], a[3].at[s, frm], a[6].at[s, frm], a[7].at[s, frm], (pi, j)).wait_recv()
                for k in range(hs):
                    state[k] += a[3][s, frm, k].astype(F32)
        for k in range(hs):
            a[4][s, r, k] = state[k].astype(BF16)
        z_copy(a, s).start()

    def gather_state(a, s):
        pair_copy(a, s, 1).wait_recv()
        rc(a[4].at[s, 1 - r], a[4].at[s, 1 - r], a[8].at[0, s], a[8].at[1, s], (pi, j)).wait_recv()
        for h in range(heads):
            at = (s, h // hs, h % hs)
            near_state = jnp.where(r == (1 if a[9] else 0), a[1][at].astype(F32), 0.0)
            state[h] = a[4][at].astype(F32) + near_state

    def end_state(a, s):
        pair_copy(a, s, 0).wait_send()
        pair_copy(a, s, 1).wait_send()
        z_copy(a, s).wait_send()
        for to in range(groups):
            @pl.when((to > g) if a[9] else (to < g))
            def _():
                group_copy(a, s, to).wait_send()

    ka = (ks_send, ks_pair, ks_sum, ks_slots, ks_z, kp, kg_s, kg_r, kz, True)
    qa = (qs_send, qs_pair, qs_sum, qs_slots, qs_z, qp, qg_s, qg_r, qz, False)

    loads[0].wait()
    loads[1].wait()
    for s in range(seqs):
        for h in range(heads):
            ks_send[s, h // hs, h % hs] = dot(k_v[s, :, lane(h)], v_v[s, :, lane(h)], 0, 0).astype(BF16)
        send_pair(ka, s)

    rows = lax.broadcasted_iota(jnp.int32, (span, span), 0)
    causal = rows >= lax.broadcasted_iota(jnp.int32, (span, span), 1)

    loads[2].wait()
    for s in range(seqs):
        for h in range(heads):
            score = dot(q_v[s, :, lane(h)], k_v[s, :, lane(h)], 1, 1)
            score = jnp.where(causal, score, 0.0).astype(BF16)
            sc[s, h] = score
            att[s, :, lane(h)] = dot(score, v_v[s, :, lane(h)], 1, 0)
        relay_p(ka, s)
    loads[3].wait()
    loads[4].wait()

    def gated(s, src, first=False):
        at = pl.ds(pl.multiple_of(src * feat, feat), feat)
        new = dot(gbuf[s, src], wo_v[:, at], 1, 1)
        if first:
            dgated[...] = new
        else:
            dgated[...] += new

    def gate_stage(s, hook):
        own_loads[s].wait()
        gated(s, j, True)
        ag_wait(s, pj)
        gated(s, pj)
        if s + 1 < seqs:
            for copy in far[s]:
                copy.wait_send()
            for copy in far[s + 1]:
                copy.start()
            near[s + 1].start()
        for x, o in enumerate(others):
            src = 2 * o + p
            ag_wait(s, src)
            rc(gbuf.at[s, src], gbuf.at[s, src], ag_f.at[s, x], ag_r.at[s, src], (i, pj)).start()
            gated(s, src)
        hook()
        for o in others:
            src = 2 * o + 1 - p
            ag_wait(s, src)
            gated(s, src)
        for h in range(heads):
            gate = jax.nn.sigmoid(g_v[s, :, lane(h)].astype(F32))
            d_out = (dgated[:, lane(h)] * gate).astype(BF16)
            dout[s, :, lane(h)] = d_out
            qs_send[s, h // hs, h % hs] = dot(q_v[s, :, lane(h)], d_out, 0, 0).astype(BF16)
        send_pair(qa, s)

    def head_stage(s, hook):
        gather_state(ka, s)
        for h in range(heads):
            if h == hs:
                hook()
            query, key, value = q_v[s, :, lane(h)], k_v[s, :, lane(h)], v_v[s, :, lane(h)]
            d_out = dout[s, :, lane(h)]
            back = jnp.where(causal, dot(d_out, value, 1, 1), 0.0).astype(BF16)
            prefix = state[h].astype(BF16)
            dq = dot(back, key, 1, 0) + dot(d_out, prefix, 1, 1)
            dcat[0, s, :, lane(h)] = (factor * dq).astype(BF16)
            dki[s, :, lane(h)] = dot(back, query, 0, 0)
            dvi[s, :, lane(h)] = dot(sc[s, h], d_out, 0, 0)
            attended = factor * (att[s, :, lane(h)] + dot(query, prefix, 1, 0))
            gate = jax.nn.sigmoid(g_v[s, :, lane(h)].astype(F32))
            d_gate = dgated[:, lane(h)] * attended * gate * (1.0 - gate)
            dcat[1, s, :, lane(h)] = d_gate.astype(BF16)

    def half(s, at, lo):
        return dot(dcat[lo, s], w_v[lo, at, :], 1, 1) + dot(dcat[lo + 1, s], w_v[lo + 1, at, :], 1, 1)

    def early(s):
        def step(t, carry):
            at = pl.ds(pl.multiple_of(t * TILE, TILE), TILE)
            acc[:, at] = half(s, at, 0)
            return carry

        lax.fori_loop(0, width // TILE, step, 0)

    def tiles(s, chunk, put):
        def step(t, carry):
            at = pl.ds(pl.multiple_of(chunk * feat + t * TILE, TILE), TILE)
            to = pl.ds(pl.multiple_of(t * TILE, TILE), TILE)
            put(to, half(s, at, 2) + acc[:, at])
            return carry

        lax.fori_loop(0, feat // TILE, step, 0)

    def part_copy(s, o):
        return rc(part_send.at[s, o], part_recv.at[s, o], ps.at[s, o], pr.at[s, o], (i, pj))

    def y_copy(s, d):
        o = others[d - 1]
        to = chips - d - 1
        return rc(y_send.at[s, d - 1], y_h.at[to, s], ys.at[s, d - 1], yr.at[s, to], (i, 2 * o + p))

    def for_partner(s, o):
        def put(to, new):
            part_send[s, o, :, to] = new.astype(BF16)

        tiles(s, 2 * o + 1 - p, put)
        part_copy(s, o).start()

    def far_stage(s, hook):
        gather_state(qa, s)
        for h in range(heads):
            suffix = state[h].astype(BF16)
            dk = dki[s, :, lane(h)] + dot(v_v[s, :, lane(h)], suffix, 1, 1)
            dv = dvi[s, :, lane(h)] + dot(k_v[s, :, lane(h)], suffix, 1, 0)
            dcat[2, s, :, lane(h)] = (factor * dk).astype(BF16)
            dcat[3, s, :, lane(h)] = (factor * dv).astype(BF16)
        for o in others:
            for_partner(s, o)
        hook()
        for d in range(1, chips):
            o = others[d - 1]
            part_copy(s, o).wait_recv()

            def put(to, new):
                y_send[s, d - 1, :, to] = (new + part_recv[s, o, :, to].astype(F32)).astype(BF16)

            tiles(s, 2 * o + p, put)
            y_copy(s, d).start()

    def near_stage(s):
        for_partner(s, c)

        def put(to, new):
            own[s, :, to] = new

        tiles(s, j, put)

    def own_copy(s):
        return pltpu.make_async_copy(own_b.at[s], own_h.at[s], ow.at[s])

    def finish(s):
        part_copy(s, c).wait_recv()
        own_b[s] = (own[s] + part_recv[s, c].astype(F32)).astype(BF16)
        own_copy(s).start()

    gate_stage(0, lambda: relay_z(ka, 0))
    head_stage(0, lambda: relay_p(qa, 0))
    relay_z(ka, 1)
    for load in loads[5:]:
        load.wait()
    early(0)
    gate_stage(1, lambda: relay_z(qa, 0))
    far_stage(0, lambda: relay_p(qa, 1))
    head_stage(1, lambda: None)
    relay_z(qa, 1)
    near_stage(0)
    early(1)
    far_stage(1, lambda: None)
    near_stage(1)
    finish(0)
    finish(1)

    for copy in far[seqs - 1]:
        copy.wait_send()
    for s in range(seqs):
        near[s].wait_send()
        for x, o in enumerate(others):
            src = 2 * o + p
            rc(gbuf.at[s, src], gbuf.at[s, src], ag_f.at[s, x], ag_r.at[s, src], (i, pj)).wait_send()
        end_state(ka, s)
        end_state(qa, s)
        for o in others:
            part_copy(s, o).wait_send()
        part_copy(s, c).wait_send()
        own_copy(s).wait()
        for d in range(1, chips):
            y_copy(s, d).wait_send()
            rc(y_send.at[s, d - 1], y_h.at[d - 1, s], ys.at[s, d - 1], yr.at[s, d - 1], (i, pj)).wait_recv()


def body(n, ns, queries, keys, values, gate_pre, grad_out, w_query, w_key, w_value, w_gate, w_out):
    seqs, span, cols = queries.shape
    feat, width = grad_out.shape[2], w_query.shape[0]
    heads, chips, groups = cols // HD, n // 2, ns // 2
    vm = pltpu.VMEM
    dma = pltpu.SemaphoreType.DMA
    tok = (seqs, span, cols)
    st = (seqs, 2, heads // 2, HD, HD)
    one = (seqs, heads // 2, HD, HD)
    slots = (seqs, groups, heads // 2, HD, HD)
    chunk = (seqs, chips, span, feat)
    scratch = [
        vm(tok, BF16), vm(tok, BF16), vm(tok, BF16), vm(tok, BF16),
        vm(w_out.shape, BF16), vm((4, width, cols), BF16),
        vm((seqs, n, span, feat), BF16),
        vm((seqs, heads, span, span), BF16), vm(tok, F32), vm((span, cols), F32),
        vm(tok, BF16), vm((4,) + tok, BF16), vm(tok, F32), vm(tok, F32), vm((span, width), F32),
        vm(st, BF16), vm(st, BF16), vm(one, BF16), vm(slots, BF16), vm(st, BF16),
        vm(st, BF16), vm(st, BF16), vm(one, BF16), vm(slots, BF16), vm(st, BF16),
        vm((heads, HD, HD), F32),
        vm(chunk, BF16), vm(chunk, BF16), vm((seqs, chips - 1, span, feat), BF16),
        vm((seqs, span, feat), F32), vm((seqs, span, feat), BF16),
        dma((9,)), dma((seqs,)), dma((seqs, chips)), dma((seqs, chips)), dma((seqs, n)),
        dma((2, seqs, 2)), dma((seqs, groups)), dma((seqs, groups)), dma((2, seqs)),
        dma((2, seqs, 2)), dma((seqs, groups)), dma((seqs, groups)), dma((2, seqs)),
        dma((seqs, chips)), dma((seqs, chips)), dma((seqs, chips)), dma((seqs, chips)), dma((seqs,)),
    ]
    flops = 2 * seqs * span * cols * width * 5
    own, far = pl.pallas_call(
        functools.partial(kernel, n, ns),
        out_shape=(
            jax.ShapeDtypeStruct((seqs, span, feat), BF16),
            jax.ShapeDtypeStruct((chips - 1, seqs, span, feat), BF16),
        ),
        in_specs=[pl.BlockSpec(memory_space=pl.ANY)] * 10,
        out_specs=[pl.BlockSpec(memory_space=pl.ANY)] * 2,
        scratch_shapes=scratch,
        cost_estimate=pl.CostEstimate(flops=flops, bytes_accessed=10 * width * cols, transcendentals=0),
        compiler_params=pltpu.CompilerParams(
            collective_id=0, has_side_effects=True, vmem_limit_bytes=58 * 1024 * 1024
        ),
    )(queries, keys, values, gate_pre, grad_out, w_query, w_key, w_value, w_gate, w_out)
    total = own.astype(F32)
    for d in range(chips - 1):
        total = total + far[d].astype(F32)
    return total.astype(BF16)


def solution(mesh):
    return jax.shard_map(
        functools.partial(body, mesh.shape["head"], mesh.shape["seq"]),
        mesh=mesh,
        in_specs=(
            P(None, "seq", "head"),
            P(None, "seq", "head"),
            P(None, "seq", "head"),
            P(None, "seq", "head"),
            P(None, "seq", "head"),
            P(None, "head"),
            P(None, "head"),
            P(None, "head"),
            P(None, "head"),
            P("head", None),
        ),
        out_specs=P(None, "seq", "head"),
        check_vma=False,
    )
```

```python
import functools

import jax
import jax.numpy as jnp
from jax import lax
from jax.experimental import pallas as pl
from jax.experimental.pallas import tpu as pltpu
from jax.sharding import PartitionSpec as P

HD = 128
TILE = 512
MESH = pl.DeviceIdType.MESH
BF16, F32 = jnp.bfloat16, jnp.float32


def dot(a, b, ca, cb):
    return lax.dot_general(a, b, (((ca,), (cb,)), ((), ())), preferred_element_type=F32)


def kernel(
    n, ns,
    q_h, k_h, v_h, g_h, go_h, wq_h, wk_h, wv_h, wg_h, wo_h, own_h, y_h,
    q_v, k_v, v_v, g_v, wo_v, w_v, gbuf, sc, att, dgated, dout, dcat, dki, dvi, acc,
    ks_send, ks_pair, ks_sum, ks_slots, ks_z, qs_send, qs_pair, qs_sum, qs_slots, qs_z, state,
    part_send, part_recv, y_send, own, own_b,
    ld, ld_own, ag_s, ag_f, ag_r, kp, kg_s, kg_r, kz, qp, qg_s, qg_r, qz, ps, pr, ys, yr, ow,
):
    seqs, span, cols = q_v.shape
    feat = go_h.shape[2]
    width = wq_h.shape[0]
    heads = cols // HD
    hs = heads // 2
    chips, groups = n // 2, ns // 2
    factor = float(ns * span) ** (-0.5)
    i, j = lax.axis_index("seq"), lax.axis_index("head")
    c, p = j // 2, lax.rem(j, 2)
    g, r = i // 2, lax.rem(i, 2)
    pj, pi = j + 1 - 2 * p, i + 1 - 2 * r
    others = [lax.rem(c + d, chips) for d in range(1, chips)]

    def rc(src, dst, ss, rs, dev):
        return pltpu.make_async_remote_copy(
            src_ref=src, dst_ref=dst, send_sem=ss, recv_sem=rs, device_id=dev, device_id_type=MESH
        )

    barrier = pltpu.get_barrier_semaphore()
    peers = [(i, pj), (pi, j)]
    peers += [(i, 2 * o + p) for o in others]
    peers += [(2 * lax.rem(g + d, groups) + r, j) for d in range(1, groups)]
    for peer in peers:
        pl.semaphore_signal(barrier, inc=1, device_id=peer, device_id_type=MESH)

    pairs = [(k_h, k_v), (v_h, v_v), (q_h, q_v), (wo_h, wo_v), (g_h, g_v)]
    pairs += [(w, w_v.at[:, pl.ds(x * cols, cols)]) for x, w in enumerate((wq_h, wg_h, wk_h, wv_h))]
    loads = [pltpu.make_async_copy(a, b, ld.at[x]) for x, (a, b) in enumerate(pairs)]
    own_loads = [pltpu.make_async_copy(go_h.at[s], gbuf.at[s, j], ld_own.at[s]) for s in range(seqs)]
    for load in loads[:4] + own_loads + loads[4:]:
        load.start()
    pl.semaphore_wait(barrier, len(peers))

    def ag_far(s):
        return [
            rc(go_h.at[s], gbuf.at[s, j], ag_s.at[s, x], ag_r.at[s, j], (i, 2 * o + p))
            for x, o in enumerate(others)
        ]

    def ag_near(s):
        return rc(go_h.at[s], gbuf.at[s, j], ag_s.at[s, chips - 1], ag_r.at[s, j], (i, pj))

    def ag_wait(s, src):
        rc(go_h.at[s], gbuf.at[s, src], ag_s.at[s, 0], ag_r.at[s, src], (i, pj)).wait_recv()

    far = [ag_far(s) for s in range(seqs)]
    near = [ag_near(s) for s in range(seqs)]
    for copy in far[0]:
        copy.start()
    near[0].start()

    def lane(h):
        return slice(h * HD, (h + 1) * HD)

    def pair_copy(a, s, m):
        half = r if m else 1 - r
        return rc(a[0].at[s, half], a[1].at[s, half], a[5].at[0, s, m], a[5].at[1, s, m], (pi, j))

    def group_copy(a, s, to):
        return rc(a[2].at[s], a[3].at[s, g], a[6].at[s, to], a[7].at[s, g], (2 * to + r, j))

    def z_copy(a, s):
        return rc(a[4].at[s, r], a[4].at[s, r], a[8].at[0, s], a[8].at[1, s], (pi, j))

    def send_pair(a, s):
        pair_copy(a, s, 0).start()
        pair_copy(a, s, 1).start()

    def relay_p(a, s):
        pair_copy(a, s, 0).wait_recv()
        for k in range(hs):
            a[2][s, k] = (a[0][s, r, k].astype(F32) + a[1][s, r, k].astype(F32)).astype(BF16)
        for to in range(groups):
            @pl.when((to > g) if a[9] else (to < g))
            def _():
                group_copy(a, s, to).start()

    def relay_z(a, s):
        for k in range(hs):
            state[k] = jnp.zeros((HD, HD), F32)
        for frm in range(groups):
            @pl.when((frm < g) if a[9] else (frm > g))
            def _():
                rc(a[2].at[s], a[3].at[s, frm], a[6].at[s, frm], a[7].at[s, frm], (pi, j)).wait_recv()
                for k in range(hs):
                    state[k] += a[3][s, frm, k].astype(F32)
        for k in range(hs):
            a[4][s, r, k] = state[k].astype(BF16)
        z_copy(a, s).start()

    def gather_state(a, s):
        pair_copy(a, s, 1).wait_recv()
        rc(a[4].at[s, 1 - r], a[4].at[s, 1 - r], a[8].at[0, s], a[8].at[1, s], (pi, j)).wait_recv()
        for h in range(heads):
            at = (s, h // hs, h % hs)
            near_state = jnp.where(r == (1 if a[9] else 0), a[1][at].astype(F32), 0.0)
            state[h] = a[4][at].astype(F32) + near_state

    def end_state(a, s):
        pair_copy(a, s, 0).wait_send()
        pair_copy(a, s, 1).wait_send()
        z_copy(a, s).wait_send()
        for to in range(groups):
            @pl.when((to > g) if a[9] else (to < g))
            def _():
                group_copy(a, s, to).wait_send()

    ka = (ks_send, ks_pair, ks_sum, ks_slots, ks_z, kp, kg_s, kg_r, kz, True)
    qa = (qs_send, qs_pair, qs_sum, qs_slots, qs_z, qp, qg_s, qg_r, qz, False)

    loads[0].wait()
    loads[1].wait()
    for s in range(seqs):
        for h in range(heads):
            ks_send[s, h // hs, h % hs] = dot(k_v[s, :, lane(h)], v_v[s, :, lane(h)], 0, 0).astype(BF16)
        send_pair(ka, s)

    rows = lax.broadcasted_iota(jnp.int32, (span, span), 0)
    causal = rows >= lax.broadcasted_iota(jnp.int32, (span, span), 1)

    loads[2].wait()
    for s in range(seqs):
        for h in range(heads):
            score = dot(q_v[s, :, lane(h)], k_v[s, :, lane(h)], 1, 1)
            score = jnp.where(causal, score, 0.0).astype(BF16)
            sc[s, h] = score
            att[s, :, lane(h)] = dot(score, v_v[s, :, lane(h)], 1, 0)
        relay_p(ka, s)
    loads[3].wait()
    loads[4].wait()

    def gated(s, src, first=False):
        at = pl.ds(pl.multiple_of(src * feat, feat), feat)
        new = dot(gbuf[s, src], wo_v[:, at], 1, 1)
        if first:
            dgated[...] = new
        else:
            dgated[...] += new

    def gate_stage(s, before, sent, after):
        own_loads[s].wait()
        gated(s, j, True)
        ag_wait(s, pj)
        gated(s, pj)
        if s + 1 < seqs:
            for copy in far[s]:
                copy.wait_send()
            for copy in far[s + 1]:
                copy.start()
            near[s + 1].start()
        before()
        for x, o in enumerate(others):
            src = 2 * o + p
            ag_wait(s, src)
            rc(gbuf.at[s, src], gbuf.at[s, src], ag_f.at[s, x], ag_r.at[s, src], (i, pj)).start()
        sent()
        for o in others:
            gated(s, 2 * o + p)
        after()
        for o in others:
            src = 2 * o + 1 - p
            ag_wait(s, src)
            gated(s, src)
        for h in range(heads):
            gate = jax.nn.sigmoid(g_v[s, :, lane(h)].astype(F32))
            d_out = (dgated[:, lane(h)] * gate).astype(BF16)
            dout[s, :, lane(h)] = d_out
            qs_send[s, h // hs, h % hs] = dot(q_v[s, :, lane(h)], d_out, 0, 0).astype(BF16)
        send_pair(qa, s)

    def head_stage(s, hook):
        gather_state(ka, s)
        for h in range(heads):
            if h == hs:
                hook()
            query, key, value = q_v[s, :, lane(h)], k_v[s, :, lane(h)], v_v[s, :, lane(h)]
            d_out = dout[s, :, lane(h)]
            back = jnp.where(causal, dot(d_out, value, 1, 1), 0.0).astype(BF16)
            prefix = state[h].astype(BF16)
            dq = dot(back, key, 1, 0) + dot(d_out, prefix, 1, 1)
            dcat[s, :, lane(0 * heads + h)] = (factor * dq).astype(BF16)
            dki[s, :, lane(h)] = dot(back, query, 0, 0)
            dvi[s, :, lane(h)] = dot(sc[s, h], d_out, 0, 0)
            attended = factor * (att[s, :, lane(h)] + dot(query, prefix, 1, 0))
            gate = jax.nn.sigmoid(g_v[s, :, lane(h)].astype(F32))
            d_gate = dgated[:, lane(h)] * attended * gate * (1.0 - gate)
            dcat[s, :, lane(1 * heads + h)] = d_gate.astype(BF16)

    tile = min(TILE, feat // 2)

    def product(s, at, lo, hi):
        lo, hi = lo * cols, hi * cols
        return dot(dcat[s, :, lo:hi], w_v[at, lo:hi], 1, 1)

    def tile_loop(step):
        def run(t, carry):
            step(t)
            return carry

        lax.fori_loop(0, feat // tile, run, 0)

    def early(s, chunk):
        def step(t):
            at = pl.ds(pl.multiple_of(chunk * feat + t * tile, tile), tile)
            acc[:, at] = product(s, at, 0, 2)

        tile_loop(step)

    def tiles(s, chunk, put, whole=False):
        def step(t):
            at = pl.ds(pl.multiple_of(chunk * feat + t * tile, tile), tile)
            to = pl.ds(pl.multiple_of(t * tile, tile), tile)
            put(to, product(s, at, 0, 4) if whole else product(s, at, 2, 4) + acc[:, at])

        tile_loop(step)

    def part_copy(s, o):
        return rc(part_send.at[s, o], part_recv.at[s, o], ps.at[s, o], pr.at[s, o], (i, pj))

    def y_copy(s, d, t):
        o = others[d - 1]
        to = chips - d - 1
        at = pl.ds(pl.multiple_of(t * tile, tile), tile)
        return rc(
            y_send.at[s, d - 1, :, at], y_h.at[to, s, :, at],
            ys.at[s, d - 1, t], yr.at[s, to, t], (i, 2 * o + p),
        )

    def for_partner(s, o, whole=False):
        def put(to, new):
            part_send[s, o, :, to] = new.astype(BF16)

        tiles(s, 2 * o + 1 - p, put, whole)
        part_copy(s, o).start()

    def far_begin(s):
        gather_state(qa, s)
        for h in range(heads):
            suffix = state[h].astype(BF16)
            dk = dki[s, :, lane(h)] + dot(v_v[s, :, lane(h)], suffix, 1, 1)
            dv = dvi[s, :, lane(h)] + dot(k_v[s, :, lane(h)], suffix, 1, 0)
            dcat[s, :, lane(2 * heads + h)] = (factor * dk).astype(BF16)
            dcat[s, :, lane(3 * heads + h)] = (factor * dv).astype(BF16)
        for o in others:
            for_partner(s, o)

    def far_end(s):
        for d in range(1, chips):
            o = others[d - 1]
            part_copy(s, o).wait_recv()

            def step(t):
                at = pl.ds(pl.multiple_of((2 * o + p) * feat + t * tile, tile), tile)
                to = pl.ds(pl.multiple_of(t * tile, tile), tile)
                new = product(s, at, 2, 4) + acc[:, at] + part_recv[s, o, :, to].astype(F32)
                y_send[s, d - 1, :, to] = new.astype(BF16)
                y_copy(s, d, t).start()

            tile_loop(step)

    def near_stage(s, whole):
        for_partner(s, c, whole)

        def put(to, new):
            own[s, :, to] = new

        tiles(s, j, put, whole)

    def own_copy(s):
        return pltpu.make_async_copy(own_b.at[s], own_h.at[s], ow.at[s])

    def finish(s):
        part_copy(s, c).wait_recv()
        own_b[s] = (own[s] + part_recv[s, c].astype(F32)).astype(BF16)
        own_copy(s).start()

    def nothing():
        return None

    gate_stage(0, nothing, nothing, lambda: relay_z(ka, 0))
    head_stage(0, lambda: relay_p(qa, 0))
    relay_z(ka, 1)
    for load in loads[5:]:
        load.wait()
    lax.fori_loop(0, n, lambda x, carry: (early(0, x), carry)[1], 0)
    gate_stage(1, lambda: relay_z(qa, 0), lambda: far_begin(0), nothing)
    far_end(0)
    relay_p(qa, 1)
    head_stage(1, nothing)
    relay_z(qa, 1)
    for o in others:
        early(1, 2 * o + 1 - p)
        early(1, 2 * o + p)
    far_begin(1)
    far_end(1)
    near_stage(0, False)
    near_stage(1, True)
    finish(0)
    finish(1)

    for copy in far[seqs - 1]:
        copy.wait_send()
    for s in range(seqs):
        near[s].wait_send()
        for x, o in enumerate(others):
            src = 2 * o + p
            rc(gbuf.at[s, src], gbuf.at[s, src], ag_f.at[s, x], ag_r.at[s, src], (i, pj)).wait_send()
        end_state(ka, s)
        end_state(qa, s)
        for o in others:
            part_copy(s, o).wait_send()
        part_copy(s, c).wait_send()
        own_copy(s).wait()
        for d in range(1, chips):
            for t in range(feat // tile):
                y_copy(s, d, t).wait_send()
                at = pl.ds(t * tile, tile)
                rc(
                    y_send.at[s, d - 1, :, at], y_h.at[d - 1, s, :, at],
                    ys.at[s, d - 1, t], yr.at[s, d - 1, t], (i, pj),
                ).wait_recv()


def body(n, ns, queries, keys, values, gate_pre, grad_out, w_query, w_key, w_value, w_gate, w_out):
    seqs, span, cols = queries.shape
    feat, width = grad_out.shape[2], w_query.shape[0]
    heads, chips, groups = cols // HD, n // 2, ns // 2
    vm = pltpu.VMEM
    dma = pltpu.SemaphoreType.DMA
    tok = (seqs, span, cols)
    st = (seqs, 2, heads // 2, HD, HD)
    one = (seqs, heads // 2, HD, HD)
    slots = (seqs, groups, heads // 2, HD, HD)
    chunk = (seqs, chips, span, feat)
    scratch = [
        vm(tok, BF16), vm(tok, BF16), vm(tok, BF16), vm(tok, BF16),
        vm(w_out.shape, BF16), vm((width, 4 * cols), BF16),
        vm((seqs, n, span, feat), BF16),
        vm((seqs, heads, span, span), BF16), vm(tok, F32), vm((span, cols), F32),
        vm(tok, BF16), vm((seqs, span, 4 * cols), BF16), vm(tok, F32), vm(tok, F32), vm((span, width), F32),
        vm(st, BF16), vm(st, BF16), vm(one, BF16), vm(slots, BF16), vm(st, BF16),
        vm(st, BF16), vm(st, BF16), vm(one, BF16), vm(slots, BF16), vm(st, BF16),
        vm((heads, HD, HD), F32),
        vm(chunk, BF16), vm(chunk, BF16), vm((seqs, chips - 1, span, feat), BF16),
        vm((seqs, span, feat), F32), vm((seqs, span, feat), BF16),
        dma((9,)), dma((seqs,)), dma((seqs, chips)), dma((seqs, chips)), dma((seqs, n)),
        dma((2, seqs, 2)), dma((seqs, groups)), dma((seqs, groups)), dma((2, seqs)),
        dma((2, seqs, 2)), dma((seqs, groups)), dma((seqs, groups)), dma((2, seqs)),
        dma((seqs, chips)), dma((seqs, chips)), dma((seqs, chips, 2)), dma((seqs, chips, 2)), dma((seqs,)),
    ]
    flops = 2 * seqs * span * cols * width * 5
    own, far = pl.pallas_call(
        functools.partial(kernel, n, ns),
        out_shape=(
            jax.ShapeDtypeStruct((seqs, span, feat), BF16),
            jax.ShapeDtypeStruct((chips - 1, seqs, span, feat), BF16),
        ),
        in_specs=[pl.BlockSpec(memory_space=pl.ANY)] * 10,
        out_specs=[pl.BlockSpec(memory_space=pl.ANY)] * 2,
        scratch_shapes=scratch,
        cost_estimate=pl.CostEstimate(flops=flops, bytes_accessed=10 * width * cols, transcendentals=0),
        compiler_params=pltpu.CompilerParams(
            collective_id=0, has_side_effects=True, vmem_limit_bytes=58 * 1024 * 1024
        ),
    )(queries, keys, values, gate_pre, grad_out, w_query, w_key, w_value, w_gate, w_out)
    total = own.astype(F32)
    for d in range(chips - 1):
        total = total + far[d].astype(F32)
    return total.astype(BF16)


def solution(mesh):
    return jax.shard_map(
        functools.partial(body, mesh.shape["head"], mesh.shape["seq"]),
        mesh=mesh,
        in_specs=(
            P(None, "seq", "head"),
            P(None, "seq", "head"),
            P(None, "seq", "head"),
            P(None, "seq", "head"),
            P(None, "seq", "head"),
            P(None, "head"),
            P(None, "head"),
            P(None, "head"),
            P(None, "head"),
            P("head", None),
        ),
        out_specs=P(None, "seq", "head"),
        check_vma=False,
    )
```

```python
import functools

import jax
import jax.numpy as jnp
from jax import lax
from jax.experimental import pallas as pl
from jax.experimental.pallas import tpu as pltpu
from jax.sharding import PartitionSpec as P

HD = 128
TILE = 512
MESH = pl.DeviceIdType.MESH
BF16, F32 = jnp.bfloat16, jnp.float32


def dot(a, b, ca, cb):
    return lax.dot_general(a, b, (((ca,), (cb,)), ((), ())), preferred_element_type=F32)


def kernel(
    n, ns,
    q_h, k_h, v_h, g_h, go_h, wq_h, wk_h, wv_h, wg_h, wo_h, own_h, y_h,
    q_v, k_v, v_v, g_v, wo_v, w_v, gbuf, sct, q_t, att, dgated, dout, dcat, dki, dvi, acc,
    ks_send, ks_pair, ks_sum, ks_slots, ks_z, qs_send, qs_pair, qs_sum, qs_slots, qs_z, state,
    part_send, part_recv, y_send, own, own_b,
    ld, ld_own, ag_s, ag_f, ag_r, kp, kg_s, kg_r, kz, qp, qg_s, qg_r, qz, ps, pr, ys, yr, ow,
):
    seqs, span, cols = q_v.shape
    feat = go_h.shape[2]
    width = wq_h.shape[0]
    heads = cols // HD
    hs = heads // 2
    chips, groups = n // 2, ns // 2
    factor = float(ns * span) ** (-0.5)
    i, j = lax.axis_index("seq"), lax.axis_index("head")
    c, p = j // 2, lax.rem(j, 2)
    g, r = i // 2, lax.rem(i, 2)
    pj, pi = j + 1 - 2 * p, i + 1 - 2 * r
    others = [lax.rem(c + d, chips) for d in range(1, chips)]

    def rc(src, dst, ss, rs, dev):
        return pltpu.make_async_remote_copy(
            src_ref=src, dst_ref=dst, send_sem=ss, recv_sem=rs, device_id=dev, device_id_type=MESH
        )

    barrier = pltpu.get_barrier_semaphore()
    peers = [(i, pj), (pi, j)]
    peers += [(i, 2 * o + p) for o in others]
    peers += [(2 * lax.rem(g + d, groups) + r, j) for d in range(1, groups)]
    for peer in peers:
        pl.semaphore_signal(barrier, inc=1, device_id=peer, device_id_type=MESH)

    pairs = [(k_h, k_v), (v_h, v_v), (q_h, q_v), (wo_h, wo_v), (g_h, g_v)]
    pairs += [(w, w_v.at[:, pl.ds(x * cols, cols)]) for x, w in enumerate((wq_h, wg_h, wk_h, wv_h))]
    loads = [pltpu.make_async_copy(a, b, ld.at[x]) for x, (a, b) in enumerate(pairs)]
    own_loads = [pltpu.make_async_copy(go_h.at[s], gbuf.at[s, j], ld_own.at[s]) for s in range(seqs)]
    for load in loads[:4] + own_loads + loads[4:]:
        load.start()
    pl.semaphore_wait(barrier, len(peers))

    def ag_far(s):
        return [
            rc(go_h.at[s], gbuf.at[s, j], ag_s.at[s, x], ag_r.at[s, j], (i, 2 * o + p))
            for x, o in enumerate(others)
        ]

    def ag_near(s):
        return rc(go_h.at[s], gbuf.at[s, j], ag_s.at[s, chips - 1], ag_r.at[s, j], (i, pj))

    def ag_wait(s, src):
        rc(go_h.at[s], gbuf.at[s, src], ag_s.at[s, 0], ag_r.at[s, src], (i, pj)).wait_recv()

    far = [ag_far(s) for s in range(seqs)]
    near = [ag_near(s) for s in range(seqs)]
    for copy in far[0]:
        copy.start()
    for copy in near:
        copy.start()

    def lane(h):
        return slice(h * HD, (h + 1) * HD)

    def pair_copy(a, s, m):
        half = r if m else 1 - r
        return rc(a[0].at[s, half], a[1].at[s, half], a[5].at[0, s, m], a[5].at[1, s, m], (pi, j))

    def group_copy(a, s, to):
        return rc(a[2].at[s], a[3].at[s, g], a[6].at[s, to], a[7].at[s, g], (2 * to + r, j))

    def z_copy(a, s):
        return rc(a[4].at[s, r], a[4].at[s, r], a[8].at[0, s], a[8].at[1, s], (pi, j))

    def send_pair(a, s):
        pair_copy(a, s, 0).start()
        pair_copy(a, s, 1).start()

    def relay_p(a, s):
        pair_copy(a, s, 0).wait_recv()
        for k in range(hs):
            a[2][s, k] = (a[0][s, r, k].astype(F32) + a[1][s, r, k].astype(F32)).astype(BF16)
        for to in range(groups):
            @pl.when((to > g) if a[9] else (to < g))
            def _():
                group_copy(a, s, to).start()

    def relay_z(a, s):
        for k in range(hs):
            state[k] = jnp.zeros((HD, HD), F32)
        for frm in range(groups):
            @pl.when((frm < g) if a[9] else (frm > g))
            def _():
                rc(a[2].at[s], a[3].at[s, frm], a[6].at[s, frm], a[7].at[s, frm], (pi, j)).wait_recv()
                for k in range(hs):
                    state[k] += a[3][s, frm, k].astype(F32)
        for k in range(hs):
            a[4][s, r, k] = state[k].astype(BF16)
        z_copy(a, s).start()

    def gather_state(a, s):
        pair_copy(a, s, 1).wait_recv()
        rc(a[4].at[s, 1 - r], a[4].at[s, 1 - r], a[8].at[0, s], a[8].at[1, s], (pi, j)).wait_recv()
        for h in range(heads):
            at = (s, h // hs, h % hs)
            near_state = jnp.where(r == (1 if a[9] else 0), a[1][at].astype(F32), 0.0)
            state[h] = a[4][at].astype(F32) + near_state

    def end_state(a, s):
        pair_copy(a, s, 0).wait_send()
        pair_copy(a, s, 1).wait_send()
        z_copy(a, s).wait_send()
        for to in range(groups):
            @pl.when((to > g) if a[9] else (to < g))
            def _():
                group_copy(a, s, to).wait_send()

    ka = (ks_send, ks_pair, ks_sum, ks_slots, ks_z, kp, kg_s, kg_r, kz, True)
    qa = (qs_send, qs_pair, qs_sum, qs_slots, qs_z, qp, qg_s, qg_r, qz, False)

    loads[0].wait()
    loads[1].wait()
    for s in range(seqs):
        for h in range(heads):
            ks_send[s, h // hs, h % hs] = dot(k_v[s, :, lane(h)], v_v[s, :, lane(h)], 0, 0).astype(BF16)
        send_pair(ka, s)

    rows = lax.broadcasted_iota(jnp.int32, (span, span), 0)
    columns = lax.broadcasted_iota(jnp.int32, (span, span), 1)
    causal, anti = rows >= columns, rows <= columns

    loads[2].wait()
    for s in range(seqs):
        for h in range(heads):
            score = dot(q_v[s, :, lane(h)], k_v[s, :, lane(h)], 1, 1)
            score = jnp.where(causal, score, 0.0).astype(BF16)
            flip = dot(k_v[s, :, lane(h)], q_v[s, :, lane(h)], 1, 1)
            sct[s, h] = jnp.where(anti, flip, 0.0).astype(BF16)
            q_t[s, h] = q_v[s, :, lane(h)].T
            att[s, :, lane(h)] = dot(score, v_v[s, :, lane(h)], 1, 0)
        relay_p(ka, s)
    loads[3].wait()
    loads[4].wait()

    def gated(s, src, first=False):
        at = pl.ds(pl.multiple_of(src * feat, feat), feat)
        new = dot(gbuf[s, src], wo_v[:, at], 1, 1)
        if first:
            dgated[s] = new
        else:
            dgated[s] += new

    def gate_stage(s, before, sent, after):
        if s + 1 < seqs:
            for copy in far[s]:
                copy.wait_send()
            for copy in far[s + 1]:
                copy.start()
        before()
        for x, o in enumerate(others):
            src = 2 * o + p
            ag_wait(s, src)
            rc(gbuf.at[s, src], gbuf.at[s, src], ag_f.at[s, x], ag_r.at[s, src], (i, pj)).start()
        sent()
        for o in others:
            gated(s, 2 * o + p)
        after()
        for o in others:
            src = 2 * o + 1 - p
            ag_wait(s, src)
            gated(s, src)
        for h in range(heads):
            gate = jax.nn.sigmoid(g_v[s, :, lane(h)].astype(F32))
            d_out = (dgated[s, :, lane(h)] * gate).astype(BF16)
            dout[s, :, lane(h)] = d_out
            qs_send[s, h // hs, h % hs] = dot(q_t[s, h], d_out, 1, 0).astype(BF16)
        send_pair(qa, s)

    def head_stage(s, hook):
        gather_state(ka, s)
        for h in range(heads):
            if h == hs:
                hook()
            query, key, value = q_v[s, :, lane(h)], k_v[s, :, lane(h)], v_v[s, :, lane(h)]
            d_out = dout[s, :, lane(h)]
            back = jnp.where(causal, dot(d_out, value, 1, 1), 0.0).astype(BF16)
            prefix = state[h].astype(BF16)
            dq = dot(back, key, 1, 0) + dot(d_out, prefix, 1, 1)
            dcat[s, :, lane(0 * heads + h)] = (factor * dq).astype(BF16)
            flip = jnp.where(anti, dot(value, d_out, 1, 1), 0.0).astype(BF16)
            dki[s, :, lane(h)] = dot(flip, query, 1, 0)
            dvi[s, :, lane(h)] = dot(sct[s, h], d_out, 1, 0)
            attended = factor * (att[s, :, lane(h)] + dot(query, prefix, 1, 0))
            gate = jax.nn.sigmoid(g_v[s, :, lane(h)].astype(F32))
            d_gate = dgated[s, :, lane(h)] * attended * gate * (1.0 - gate)
            dcat[s, :, lane(1 * heads + h)] = d_gate.astype(BF16)

    tile = min(TILE, feat // 2)

    def product(s, at, lo, hi):
        lo, hi = lo * cols, hi * cols
        return dot(dcat[s, :, lo:hi], w_v[at, lo:hi], 1, 1)

    def tile_loop(step):
        def run(t, carry):
            step(t)
            return carry

        lax.fori_loop(0, feat // tile, run, 0)

    def early(s, chunk):
        def step(t):
            at = pl.ds(pl.multiple_of(chunk * feat + t * tile, tile), tile)
            acc[:, at] = product(s, at, 0, 2)

        tile_loop(step)

    def tiles(s, chunk, put, whole=False):
        def step(t):
            at = pl.ds(pl.multiple_of(chunk * feat + t * tile, tile), tile)
            to = pl.ds(pl.multiple_of(t * tile, tile), tile)
            put(to, product(s, at, 0, 4) if whole else product(s, at, 2, 4) + acc[:, at])

        tile_loop(step)

    def part_copy(s, o, t):
        at = pl.ds(pl.multiple_of(t * tile, tile), tile)
        return rc(
            part_send.at[s, o, :, at], part_recv.at[s, o, :, at], ps.at[s, o, t], pr.at[s, o, t], (i, pj)
        )

    def near_copy(s):
        return rc(part_send.at[s, c], part_recv.at[s, c], ps.at[s, c, 0], pr.at[s, c, 0], (i, pj))

    def y_copy(s, d, t):
        o = others[d - 1]
        to = chips - d - 1
        at = pl.ds(pl.multiple_of(t * tile, tile), tile)
        return rc(
            y_send.at[s, d - 1, :, at], y_h.at[to, s, :, at],
            ys.at[s, d - 1, t], yr.at[s, to, t], (i, 2 * o + p),
        )

    def for_partner(s, o):
        def step(t):
            at = pl.ds(pl.multiple_of((2 * o + 1 - p) * feat + t * tile, tile), tile)
            to = pl.ds(pl.multiple_of(t * tile, tile), tile)
            part_send[s, o, :, to] = (product(s, at, 2, 4) + acc[:, at]).astype(BF16)
            part_copy(s, o, t).start()

        tile_loop(step)

    def far_begin(s):
        gather_state(qa, s)
        for h in range(heads):
            suffix = state[h].astype(BF16)
            dk = dki[s, :, lane(h)] + dot(v_v[s, :, lane(h)], suffix, 1, 1)
            dv = dvi[s, :, lane(h)] + dot(k_v[s, :, lane(h)], suffix, 1, 0)
            dcat[s, :, lane(2 * heads + h)] = (factor * dk).astype(BF16)
            dcat[s, :, lane(3 * heads + h)] = (factor * dv).astype(BF16)
        for o in others:
            for_partner(s, o)

    def far_end(s):
        for d in range(1, chips):
            o = others[d - 1]
            def step(t):
                part_copy(s, o, t).wait_recv()
                at = pl.ds(pl.multiple_of((2 * o + p) * feat + t * tile, tile), tile)
                to = pl.ds(pl.multiple_of(t * tile, tile), tile)
                new = product(s, at, 2, 4) + acc[:, at] + part_recv[s, o, :, to].astype(F32)
                y_send[s, d - 1, :, to] = new.astype(BF16)
                y_copy(s, d, t).start()

            tile_loop(step)

    def near_stage(s, whole):
        def put(to, new):
            part_send[s, c, :, to] = new.astype(BF16)

        tiles(s, pj, put, whole)
        near_copy(s).start()

        def put(to, new):
            own[s, :, to] = new

        tiles(s, j, put, True)

    def own_copy(s):
        return pltpu.make_async_copy(own_b.at[s], own_h.at[s], ow.at[s])

    def finish(s):
        near_copy(s).wait_recv()
        own_b[s] = (own[s] + part_recv[s, c].astype(F32)).astype(BF16)
        own_copy(s).start()

    for s in range(seqs):
        own_loads[s].wait()
        gated(s, j, True)
        ag_wait(s, pj)
        gated(s, pj)

    def nothing():
        return None

    gate_stage(0, nothing, nothing, lambda: relay_z(ka, 0))
    head_stage(0, lambda: relay_p(qa, 0))
    relay_z(ka, 1)
    for load in loads[5:]:
        load.wait()
    for o in others:
        early(0, 2 * o + 1 - p)
        early(0, 2 * o + p)
    early(0, pj)
    gate_stage(1, lambda: relay_z(qa, 0), lambda: far_begin(0), nothing)
    far_end(0)
    relay_p(qa, 1)
    head_stage(1, nothing)
    relay_z(qa, 1)
    for o in others:
        early(1, 2 * o + 1 - p)
        early(1, 2 * o + p)
    far_begin(1)
    far_end(1)
    near_stage(0, False)
    near_stage(1, True)
    finish(0)
    finish(1)

    for copy in far[seqs - 1]:
        copy.wait_send()
    for s in range(seqs):
        near[s].wait_send()
        for x, o in enumerate(others):
            src = 2 * o + p
            rc(gbuf.at[s, src], gbuf.at[s, src], ag_f.at[s, x], ag_r.at[s, src], (i, pj)).wait_send()
        end_state(ka, s)
        end_state(qa, s)
        for o in others:
            for t in range(feat // tile):
                part_copy(s, o, t).wait_send()
        near_copy(s).wait_send()
        own_copy(s).wait()
        for d in range(1, chips):
            for t in range(feat // tile):
                y_copy(s, d, t).wait_send()
                at = pl.ds(t * tile, tile)
                rc(
                    y_send.at[s, d - 1, :, at], y_h.at[d - 1, s, :, at],
                    ys.at[s, d - 1, t], yr.at[s, d - 1, t], (i, pj),
                ).wait_recv()


def body(n, ns, queries, keys, values, gate_pre, grad_out, w_query, w_key, w_value, w_gate, w_out):
    seqs, span, cols = queries.shape
    feat, width = grad_out.shape[2], w_query.shape[0]
    heads, chips, groups = cols // HD, n // 2, ns // 2
    vm = pltpu.VMEM
    dma = pltpu.SemaphoreType.DMA
    tok = (seqs, span, cols)
    st = (seqs, 2, heads // 2, HD, HD)
    one = (seqs, heads // 2, HD, HD)
    slots = (seqs, groups, heads // 2, HD, HD)
    chunk = (seqs, chips, span, feat)
    scratch = [
        vm(tok, BF16), vm(tok, BF16), vm(tok, BF16), vm(tok, BF16),
        vm(w_out.shape, BF16), vm((width, 4 * cols), BF16),
        vm((seqs, n, span, feat), BF16),
        vm((seqs, heads, span, span), BF16), vm((seqs, heads, HD, span), BF16), vm(tok, F32), vm(tok, F32),
        vm(tok, BF16), vm((seqs, span, 4 * cols), BF16), vm(tok, F32), vm(tok, F32), vm((span, width), F32),
        vm(st, BF16), vm(st, BF16), vm(one, BF16), vm(slots, BF16), vm(st, BF16),
        vm(st, BF16), vm(st, BF16), vm(one, BF16), vm(slots, BF16), vm(st, BF16),
        vm((heads, HD, HD), F32),
        vm(chunk, BF16), vm(chunk, BF16), vm((seqs, chips - 1, span, feat), BF16),
        vm((seqs, span, feat), F32), vm((seqs, span, feat), BF16),
        dma((9,)), dma((seqs,)), dma((seqs, chips)), dma((seqs, chips)), dma((seqs, n)),
        dma((2, seqs, 2)), dma((seqs, groups)), dma((seqs, groups)), dma((2, seqs)),
        dma((2, seqs, 2)), dma((seqs, groups)), dma((seqs, groups)), dma((2, seqs)),
        dma((seqs, chips, 2)), dma((seqs, chips, 2)), dma((seqs, chips, 2)), dma((seqs, chips, 2)), dma((seqs,)),
    ]
    flops = 2 * seqs * span * cols * width * 5
    own, far = pl.pallas_call(
        functools.partial(kernel, n, ns),
        out_shape=(
            jax.ShapeDtypeStruct((seqs, span, feat), BF16),
            jax.ShapeDtypeStruct((chips - 1, seqs, span, feat), BF16),
        ),
        in_specs=[pl.BlockSpec(memory_space=pl.ANY)] * 10,
        out_specs=[pl.BlockSpec(memory_space=pl.ANY)] * 2,
        scratch_shapes=scratch,
        cost_estimate=pl.CostEstimate(flops=flops, bytes_accessed=10 * width * cols, transcendentals=0),
        compiler_params=pltpu.CompilerParams(
            collective_id=0, has_side_effects=True, vmem_limit_bytes=58 * 1024 * 1024
        ),
    )(queries, keys, values, gate_pre, grad_out, w_query, w_key, w_value, w_gate, w_out)
    total = own.astype(F32)
    for d in range(chips - 1):
        total = total + far[d].astype(F32)
    return total.astype(BF16)


def solution(mesh):
    return jax.shard_map(
        functools.partial(body, mesh.shape["head"], mesh.shape["seq"]),
        mesh=mesh,
        in_specs=(
            P(None, "seq", "head"),
            P(None, "seq", "head"),
            P(None, "seq", "head"),
            P(None, "seq", "head"),
            P(None, "seq", "head"),
            P(None, "head"),
            P(None, "head"),
            P(None, "head"),
            P(None, "head"),
            P("head", None),
        ),
        out_specs=P(None, "seq", "head"),
        check_vma=False,
    )
```

```python
import functools

import jax
import jax.numpy as jnp
from jax import lax
from jax.experimental import pallas as pl
from jax.experimental.pallas import tpu as pltpu
from jax.sharding import PartitionSpec as P

HD = 128
TILE = 512
MESH = pl.DeviceIdType.MESH
BF16, F32 = jnp.bfloat16, jnp.float32


def dot(a, b, ca, cb):
    return lax.dot_general(a, b, (((ca,), (cb,)), ((), ())), preferred_element_type=F32)


def kernel(
    n, ns,
    q_h, k_h, v_h, g_h, go_h, wq_h, wk_h, wv_h, wg_h, wo_h, own_h, y_h,
    q_v, k_v, v_v, g_v, wo_v, w_v, gbuf, sct, q_t, att, dgated, opened, dout, dcat, dki, dvi, acc,
    ks_send, ks_pair, ks_sum, ks_slots, ks_z, qs_send, qs_pair, qs_sum, qs_slots, qs_z, state,
    part_send, part_recv, y_send, own, own_b,
    ld, ld_own, ag_s, ag_f, ag_r, kp, kg_s, kg_r, kz, qp, qg_s, qg_r, qz, ps, pr, ys, yr, ow,
):
    seqs, span, cols = q_v.shape
    feat = go_h.shape[2]
    width = wq_h.shape[0]
    heads = cols // HD
    hs = heads // 2
    chips, groups = n // 2, ns // 2
    factor = float(ns * span) ** (-0.5)
    i, j = lax.axis_index("seq"), lax.axis_index("head")
    c, p = j // 2, lax.rem(j, 2)
    g, r = i // 2, lax.rem(i, 2)
    pj, pi = j + 1 - 2 * p, i + 1 - 2 * r
    others = [lax.rem(c + d, chips) for d in range(1, chips)]

    def rc(src, dst, ss, rs, dev):
        return pltpu.make_async_remote_copy(
            src_ref=src, dst_ref=dst, send_sem=ss, recv_sem=rs, device_id=dev, device_id_type=MESH
        )

    barrier = pltpu.get_barrier_semaphore()
    peers = [(i, pj), (pi, j)]
    peers += [(i, 2 * o + p) for o in others]
    peers += [(2 * lax.rem(g + d, groups) + r, j) for d in range(1, groups)]
    for peer in peers:
        pl.semaphore_signal(barrier, inc=1, device_id=peer, device_id_type=MESH)

    pairs = [(k_h, k_v), (v_h, v_v), (q_h, q_v), (wo_h, wo_v), (g_h, g_v)]
    pairs += [(w, w_v.at[:, pl.ds(x * cols, cols)]) for x, w in enumerate((wq_h, wg_h, wk_h, wv_h))]
    loads = [pltpu.make_async_copy(a, b, ld.at[x]) for x, (a, b) in enumerate(pairs)]
    own_loads = [pltpu.make_async_copy(go_h.at[s], gbuf.at[s, j], ld_own.at[s]) for s in range(seqs)]
    for load in loads[:4] + own_loads + loads[4:]:
        load.start()
    pl.semaphore_wait(barrier, len(peers))

    def ag_far(s):
        return [
            rc(go_h.at[s], gbuf.at[s, j], ag_s.at[s, x], ag_r.at[s, j], (i, 2 * o + p))
            for x, o in enumerate(others)
        ]

    def ag_near(s):
        return rc(go_h.at[s], gbuf.at[s, j], ag_s.at[s, chips - 1], ag_r.at[s, j], (i, pj))

    def ag_wait(s, src):
        rc(go_h.at[s], gbuf.at[s, src], ag_s.at[s, 0], ag_r.at[s, src], (i, pj)).wait_recv()

    far = [ag_far(s) for s in range(seqs)]
    near = [ag_near(s) for s in range(seqs)]
    for copy in far[0]:
        copy.start()
    for copy in near:
        copy.start()

    def lane(h):
        return slice(h * HD, (h + 1) * HD)

    def pair_copy(a, s, m):
        half = r if m else 1 - r
        return rc(a[0].at[s, half], a[1].at[s, half], a[5].at[0, s, m], a[5].at[1, s, m], (pi, j))

    def group_copy(a, s, to):
        return rc(a[2].at[s], a[3].at[s, g], a[6].at[s, to], a[7].at[s, g], (2 * to + r, j))

    def z_copy(a, s):
        return rc(a[4].at[s, r], a[4].at[s, r], a[8].at[0, s], a[8].at[1, s], (pi, j))

    def send_pair(a, s):
        pair_copy(a, s, 0).start()
        pair_copy(a, s, 1).start()

    def relay_p(a, s):
        pair_copy(a, s, 0).wait_recv()
        for k in range(hs):
            a[2][s, k] = (a[0][s, r, k].astype(F32) + a[1][s, r, k].astype(F32)).astype(BF16)
        for to in range(groups):
            @pl.when((to > g) if a[9] else (to < g))
            def _():
                group_copy(a, s, to).start()

    def relay_z(a, s):
        for k in range(hs):
            state[k] = jnp.zeros((HD, HD), F32)
        for frm in range(groups):
            @pl.when((frm < g) if a[9] else (frm > g))
            def _():
                rc(a[2].at[s], a[3].at[s, frm], a[6].at[s, frm], a[7].at[s, frm], (pi, j)).wait_recv()
                for k in range(hs):
                    state[k] += a[3][s, frm, k].astype(F32)
        for k in range(hs):
            a[4][s, r, k] = state[k].astype(BF16)
        z_copy(a, s).start()

    def gather_state(a, s):
        pair_copy(a, s, 1).wait_recv()
        rc(a[4].at[s, 1 - r], a[4].at[s, 1 - r], a[8].at[0, s], a[8].at[1, s], (pi, j)).wait_recv()
        for h in range(heads):
            at = (s, h // hs, h % hs)
            near_state = jnp.where(r == (1 if a[9] else 0), a[1][at].astype(F32), 0.0)
            state[h] = a[4][at].astype(F32) + near_state

    def end_state(a, s):
        pair_copy(a, s, 0).wait_send()
        pair_copy(a, s, 1).wait_send()
        z_copy(a, s).wait_send()
        for to in range(groups):
            @pl.when((to > g) if a[9] else (to < g))
            def _():
                group_copy(a, s, to).wait_send()

    ka = (ks_send, ks_pair, ks_sum, ks_slots, ks_z, kp, kg_s, kg_r, kz, True)
    qa = (qs_send, qs_pair, qs_sum, qs_slots, qs_z, qp, qg_s, qg_r, qz, False)

    loads[0].wait()
    loads[1].wait()
    for s in range(seqs):
        for h in range(heads):
            ks_send[s, h // hs, h % hs] = dot(k_v[s, :, lane(h)], v_v[s, :, lane(h)], 0, 0).astype(BF16)
        send_pair(ka, s)

    rows = lax.broadcasted_iota(jnp.int32, (span, span), 0)
    columns = lax.broadcasted_iota(jnp.int32, (span, span), 1)
    causal, anti = rows >= columns, rows <= columns

    loads[2].wait()
    for s in range(seqs):
        for h in range(heads):
            score = dot(q_v[s, :, lane(h)], k_v[s, :, lane(h)], 1, 1)
            score = jnp.where(causal, score, 0.0).astype(BF16)
            flip = dot(k_v[s, :, lane(h)], q_v[s, :, lane(h)], 1, 1)
            sct[s, h] = jnp.where(anti, flip, 0.0).astype(BF16)
            q_t[s, h] = q_v[s, :, lane(h)].T
            att[s, :, lane(h)] = dot(score, v_v[s, :, lane(h)], 1, 0)
        relay_p(ka, s)
    loads[3].wait()
    loads[4].wait()

    def gated(s, src, first=False):
        at = pl.ds(pl.multiple_of(src * feat, feat), feat)
        new = dot(gbuf[s, src], wo_v[:, at], 1, 1)
        if first:
            dgated[s] = new
        else:
            dgated[s] += new

    def gate_stage(s, before, sent, after):
        if s + 1 < seqs:
            for copy in far[s]:
                copy.wait_send()
            for copy in far[s + 1]:
                copy.start()
        opened[s] = jax.nn.sigmoid(g_v[s].astype(F32))
        before()
        for x, o in enumerate(others):
            src = 2 * o + p
            ag_wait(s, src)
            rc(gbuf.at[s, src], gbuf.at[s, src], ag_f.at[s, x], ag_r.at[s, src], (i, pj)).start()
        sent()
        for o in others:
            gated(s, 2 * o + p)
        after()
        for o in others:
            src = 2 * o + 1 - p
            ag_wait(s, src)
            gated(s, src)
        for h in range(heads):
            gate = opened[s, :, lane(h)]
            d_out = (dgated[s, :, lane(h)] * gate).astype(BF16)
            dout[s, :, lane(h)] = d_out
            qs_send[s, h // hs, h % hs] = dot(q_t[s, h], d_out, 1, 0).astype(BF16)
        send_pair(qa, s)

    def head_stage(s, hook):
        gather_state(ka, s)
        for h in range(heads):
            if h == hs:
                hook()
            query, key, value = q_v[s, :, lane(h)], k_v[s, :, lane(h)], v_v[s, :, lane(h)]
            d_out = dout[s, :, lane(h)]
            back = jnp.where(causal, dot(d_out, value, 1, 1), 0.0).astype(BF16)
            prefix = state[h].astype(BF16)
            dq = dot(back, key, 1, 0) + dot(d_out, prefix, 1, 1)
            dcat[s, :, lane(0 * heads + h)] = (factor * dq).astype(BF16)
            flip = jnp.where(anti, dot(value, d_out, 1, 1), 0.0).astype(BF16)
            dki[s, :, lane(h)] = dot(flip, query, 1, 0)
            dvi[s, :, lane(h)] = dot(sct[s, h], d_out, 1, 0)
            attended = factor * (att[s, :, lane(h)] + dot(query, prefix, 1, 0))
            gate = opened[s, :, lane(h)]
            d_gate = dgated[s, :, lane(h)] * attended * gate * (1.0 - gate)
            dcat[s, :, lane(1 * heads + h)] = d_gate.astype(BF16)

    tile = min(TILE, feat // 2)

    def product(s, at, lo, hi):
        lo, hi = lo * cols, hi * cols
        return dot(dcat[s, :, lo:hi], w_v[at, lo:hi], 1, 1)

    def tile_loop(step):
        def run(t, carry):
            step(t)
            return carry

        lax.fori_loop(0, feat // tile, run, 0)

    def early(s, chunk):
        def step(t):
            at = pl.ds(pl.multiple_of(chunk * feat + t * tile, tile), tile)
            acc[:, at] = product(s, at, 0, 2)

        tile_loop(step)

    def tiles(s, chunk, put, whole=False):
        def step(t):
            at = pl.ds(pl.multiple_of(chunk * feat + t * tile, tile), tile)
            to = pl.ds(pl.multiple_of(t * tile, tile), tile)
            put(to, product(s, at, 0, 4) if whole else product(s, at, 2, 4) + acc[:, at])

        tile_loop(step)

    def part_copy(s, o, t):
        at = pl.ds(pl.multiple_of(t * tile, tile), tile)
        return rc(
            part_send.at[s, o, :, at], part_recv.at[s, o, :, at], ps.at[s, o, t], pr.at[s, o, t], (i, pj)
        )

    def near_copy(s):
        return rc(part_send.at[s, c], part_recv.at[s, c], ps.at[s, c, 0], pr.at[s, c, 0], (i, pj))

    def y_copy(s, d, t):
        o = others[d - 1]
        to = chips - d - 1
        at = pl.ds(pl.multiple_of(t * tile, tile), tile)
        return rc(
            y_send.at[s, d - 1, :, at], y_h.at[to, s, :, at],
            ys.at[s, d - 1, t], yr.at[s, to, t], (i, 2 * o + p),
        )

    def for_partner(s, o):
        def step(t):
            at = pl.ds(pl.multiple_of((2 * o + 1 - p) * feat + t * tile, tile), tile)
            to = pl.ds(pl.multiple_of(t * tile, tile), tile)
            part_send[s, o, :, to] = (product(s, at, 2, 4) + acc[:, at]).astype(BF16)
            part_copy(s, o, t).start()

        tile_loop(step)

    def far_begin(s):
        gather_state(qa, s)
        for h in range(heads):
            suffix = state[h].astype(BF16)
            dk = dki[s, :, lane(h)] + dot(v_v[s, :, lane(h)], suffix, 1, 1)
            dv = dvi[s, :, lane(h)] + dot(k_v[s, :, lane(h)], suffix, 1, 0)
            dcat[s, :, lane(2 * heads + h)] = (factor * dk).astype(BF16)
            dcat[s, :, lane(3 * heads + h)] = (factor * dv).astype(BF16)
        for o in others:
            for_partner(s, o)

    def far_end(s):
        for d in range(1, chips):
            o = others[d - 1]
            def step(t):
                part_copy(s, o, t).wait_recv()
                at = pl.ds(pl.multiple_of((2 * o + p) * feat + t * tile, tile), tile)
                to = pl.ds(pl.multiple_of(t * tile, tile), tile)
                new = product(s, at, 2, 4) + acc[:, at] + part_recv[s, o, :, to].astype(F32)
                y_send[s, d - 1, :, to] = new.astype(BF16)
                y_copy(s, d, t).start()

            tile_loop(step)

    def near_stage(s, whole):
        def put(to, new):
            part_send[s, c, :, to] = new.astype(BF16)

        tiles(s, pj, put, whole)
        near_copy(s).start()

        def put(to, new):
            own[s, :, to] = new

        tiles(s, j, put, True)

    def own_copy(s):
        return pltpu.make_async_copy(own_b.at[s], own_h.at[s], ow.at[s])

    def finish(s):
        near_copy(s).wait_recv()
        own_b[s] = (own[s] + part_recv[s, c].astype(F32)).astype(BF16)
        own_copy(s).start()

    for s in range(seqs):
        own_loads[s].wait()
        gated(s, j, True)
        ag_wait(s, pj)
        gated(s, pj)

    def nothing():
        return None

    gate_stage(0, nothing, nothing, lambda: relay_z(ka, 0))
    head_stage(0, lambda: relay_p(qa, 0))
    relay_z(ka, 1)
    for load in loads[5:]:
        load.wait()
    for o in others:
        early(0, 2 * o + 1 - p)
        early(0, 2 * o + p)
    early(0, pj)
    gate_stage(1, lambda: relay_z(qa, 0), lambda: far_begin(0), nothing)
    far_end(0)
    relay_p(qa, 1)
    head_stage(1, nothing)
    relay_z(qa, 1)
    for o in others:
        early(1, 2 * o + 1 - p)
        early(1, 2 * o + p)
    far_begin(1)
    far_end(1)
    near_stage(0, False)
    near_stage(1, True)
    finish(0)
    finish(1)

    for copy in far[seqs - 1]:
        copy.wait_send()
    for s in range(seqs):
        near[s].wait_send()
        for x, o in enumerate(others):
            src = 2 * o + p
            rc(gbuf.at[s, src], gbuf.at[s, src], ag_f.at[s, x], ag_r.at[s, src], (i, pj)).wait_send()
        end_state(ka, s)
        end_state(qa, s)
        for o in others:
            for t in range(feat // tile):
                part_copy(s, o, t).wait_send()
        near_copy(s).wait_send()
        own_copy(s).wait()
        for d in range(1, chips):
            for t in range(feat // tile):
                y_copy(s, d, t).wait_send()
                at = pl.ds(t * tile, tile)
                rc(
                    y_send.at[s, d - 1, :, at], y_h.at[d - 1, s, :, at],
                    ys.at[s, d - 1, t], yr.at[s, d - 1, t], (i, pj),
                ).wait_recv()


def body(n, ns, queries, keys, values, gate_pre, grad_out, w_query, w_key, w_value, w_gate, w_out):
    seqs, span, cols = queries.shape
    feat, width = grad_out.shape[2], w_query.shape[0]
    heads, chips, groups = cols // HD, n // 2, ns // 2
    vm = pltpu.VMEM
    dma = pltpu.SemaphoreType.DMA
    tok = (seqs, span, cols)
    st = (seqs, 2, heads // 2, HD, HD)
    one = (seqs, heads // 2, HD, HD)
    slots = (seqs, groups, heads // 2, HD, HD)
    chunk = (seqs, chips, span, feat)
    scratch = [
        vm(tok, BF16), vm(tok, BF16), vm(tok, BF16), vm(tok, BF16),
        vm(w_out.shape, BF16), vm((width, 4 * cols), BF16),
        vm((seqs, n, span, feat), BF16),
        vm((seqs, heads, span, span), BF16), vm((seqs, heads, HD, span), BF16), vm(tok, F32), vm(tok, F32), vm(tok, F32),
        vm(tok, BF16), vm((seqs, span, 4 * cols), BF16), vm(tok, F32), vm(tok, F32), vm((span, width), F32),
        vm(st, BF16), vm(st, BF16), vm(one, BF16), vm(slots, BF16), vm(st, BF16),
        vm(st, BF16), vm(st, BF16), vm(one, BF16), vm(slots, BF16), vm(st, BF16),
        vm((heads, HD, HD), F32),
        vm(chunk, BF16), vm(chunk, BF16), vm((seqs, chips - 1, span, feat), BF16),
        vm((seqs, span, feat), F32), vm((seqs, span, feat), BF16),
        dma((9,)), dma((seqs,)), dma((seqs, chips)), dma((seqs, chips)), dma((seqs, n)),
        dma((2, seqs, 2)), dma((seqs, groups)), dma((seqs, groups)), dma((2, seqs)),
        dma((2, seqs, 2)), dma((seqs, groups)), dma((seqs, groups)), dma((2, seqs)),
        dma((seqs, chips, 2)), dma((seqs, chips, 2)), dma((seqs, chips, 2)), dma((seqs, chips, 2)), dma((seqs,)),
    ]
    flops = 2 * seqs * span * cols * width * 5
    own, far = pl.pallas_call(
        functools.partial(kernel, n, ns),
        out_shape=(
            jax.ShapeDtypeStruct((seqs, span, feat), BF16),
            jax.ShapeDtypeStruct((chips - 1, seqs, span, feat), BF16),
        ),
        in_specs=[pl.BlockSpec(memory_space=pl.ANY)] * 10,
        out_specs=[pl.BlockSpec(memory_space=pl.ANY)] * 2,
        scratch_shapes=scratch,
        cost_estimate=pl.CostEstimate(flops=flops, bytes_accessed=10 * width * cols, transcendentals=0),
        compiler_params=pltpu.CompilerParams(
            collective_id=0, has_side_effects=True, vmem_limit_bytes=58 * 1024 * 1024
        ),
    )(queries, keys, values, gate_pre, grad_out, w_query, w_key, w_value, w_gate, w_out)
    total = own.astype(F32)
    for d in range(chips - 1):
        total = total + far[d].astype(F32)
    return total.astype(BF16)


def solution(mesh):
    return jax.shard_map(
        functools.partial(body, mesh.shape["head"], mesh.shape["seq"]),
        mesh=mesh,
        in_specs=(
            P(None, "seq", "head"),
            P(None, "seq", "head"),
            P(None, "seq", "head"),
            P(None, "seq", "head"),
            P(None, "seq", "head"),
            P(None, "head"),
            P(None, "head"),
            P(None, "head"),
            P(None, "head"),
            P("head", None),
        ),
        out_specs=P(None, "seq", "head"),
        check_vma=False,
    )
```
